128 devices in a mesh: feat: 8 (over z, core), bulk: 16 (over y, x).
Axes of the slice: x: 4, y: 4, z: 4, core: 2. Of those that a mesh axis runs over, the one named last changes fastest.
Arguments:
- features: bfloat16 [262144, 4096], P('bulk', 'feat'), may hold values from -6 to 6
- project: bfloat16 [4096, 256], P('feat'), may hold values from -0.09375 to 0.09375
- bias: float32 [256], replicated, may hold values from -3 to 3
- send_rows: int32 [128, 128, 64], P(('feat', 'bulk')), may hold values from 0 to 2047
- send_count: int32 [128, 128], P(('feat', 'bulk')), may hold values from 0 to 64, as said below
- block_ids: int32 [128, 16, 12], P(('feat', 'bulk')), may hold values from 0 to 79, as said below
- block_weights: bfloat16 [128, 16, 12, 128, 128], P(('feat', 'bulk')), may hold values from 0 to 0.039794922
Outputs:
- node_states: bfloat16 [262144, 256], P(('bulk', 'feat'))
The draws below stay inside these ranges and needn't reach their ends.
Inputs may be any that keep to these rules, and one draw needn't show every extreme that they name: `send_rows`: entries at or past a pair's count are valid row numbers that are not sent. `send_count`: some pair of devices has exactly 64 live rows. `block_ids`: the 12 blocks of one tile differ, and the tiles of one device together name every block of its buffer.
All inputs are finite; a program needn't handle non-finite values.
Results may differ from the reference program's by a relative error of at most 0.017.
Values may be sent and summed in bfloat16 or wider, within the bound.
A program may use at most 128 MiB of HBM per device.

```python
import jax
import jax.numpy as jnp
from jax import lax

F = 4096
HID = 256
DST = 2048
CAP = 64
K = 12
BLK = 128
NODES = 262144
TILES = 16
NBLK = 80
N_FEAT = 8
N_BULK = 16
DEVICES = 128


def draw_send_count(key, part):
    key = jax.random.fold_in(key, 11)
    counts = jax.random.randint(key, (DEVICES, DEVICES), 0, CAP + 1)
    sender = jnp.arange(DEVICES)[:, None]
    target = jnp.arange(DEVICES)[None, :]
    return jnp.where(target == (sender + 1) % DEVICES, CAP, counts).astype(jnp.int32)


def block_order(key):
    return jax.random.permutation(key, NBLK)


def draw_block_ids(key, part):
    key = jax.random.fold_in(key, 23)
    keys = jax.random.split(key, DEVICES)
    orders = jax.vmap(block_order)(keys)
    places = (jnp.arange(TILES)[:, None] * K + jnp.arange(K)[None, :]) % NBLK
    return orders[:, places].astype(jnp.int32)


def with_ends(drawn, key, least, high):
    longest = drawn.shape.index(max(drawn.shape))
    spots = []
    for shift in (0, 1):
        where = [jax.random.randint(jax.random.fold_in(key, axis), (), 0, length) for axis, length in enumerate(drawn.shape)]
        where[longest] = (where[longest] + shift) % drawn.shape[longest]
        spots.append(tuple(where))
    return drawn.at[spots[0]].set(least).at[spots[1]].set(high)


def spiked(drawn, own_key, source, target, parts, factor):
    owner, partner = [(jnp.arange(drawn.shape[position]) // (drawn.shape[position] // parts)).reshape([-1 if axis == position else 1 for axis in range(drawn.ndim)]) for position in (source, target)]
    chosen = jax.random.permutation(own_key, parts)[partner]
    strong = (owner == chosen) | (owner == (partner + parts // 2) % parts)
    return jnp.where(strong, factor * drawn, drawn)


def block_levels(own_key, dims, cuts, least, high):
    factor_of, own = 1.0, jax.random.fold_in(own_key, 6)
    for axis_at, blocks in cuts:
        draws = jnp.exp(jax.random.uniform(jax.random.fold_in(own, axis_at), (blocks,), jnp.float32, least / len(cuts), high / len(cuts)))
        factor_of = factor_of * jnp.repeat(draws, dims[axis_at] // blocks).reshape([-1 if axis == axis_at else 1 for axis in range(len(dims))])
    return factor_of


def noise(key, extent, scale, reach, cuts=(), held_as=jnp.bfloat16):
    result = scale * jax.random.normal(key, extent, jnp.float32)
    if cuts:
        result = result * block_levels(key, extent, cuts, -0.22, 0.18)
    return jnp.clip(result, -reach, reach).astype(held_as)


def bell_draw_with(rng, shape, scale, limit, cuts, heavy, kind=jnp.bfloat16):
    values = scale * jax.random.normal(rng, shape, jnp.float32)
    if cuts:
        values = values * block_levels(rng, shape, cuts, -0.22, 0.18)
    return jnp.clip(spiked(values, jax.random.fold_in(rng, 3), *heavy), -limit, limit).astype(kind)


def setup_inputs(seed: int = 0) -> dict:
    splits = jax.random.split(jax.random.key(seed), 8)
    return {
        "features": bell_draw_with(splits[0], (NODES, F), 1.0, 6.0, ((0, 16), (1, 8)), (1, 0, 16, 2.0)),
        "project": noise(splits[1], (F, HID), F ** -0.5, 0.09375, ((0, 8),)),
        "bias": noise(splits[2], (HID,), 0.5, 3.0, (), jnp.float32),
        "send_rows": with_ends(jax.random.randint(splits[3], (DEVICES, DEVICES, CAP), 0, DST), jax.random.fold_in(splits[3], 1), 0, DST - 1).astype(jnp.int32),
        "send_count": draw_send_count(jax.random.fold_in(splits[7], 71), 0),
        "block_ids": draw_block_ids(jax.random.fold_in(splits[7], 71), 0),
        "block_weights": jnp.clip(0.039794922 * jax.random.uniform(splits[6], (DEVICES, TILES, K, BLK, BLK), jnp.float32) ** block_levels(splits[6], (DEVICES, TILES, K, BLK, BLK), ((0, 128),), -0.2, 0.2), 0.0, 0.039794922).astype(jnp.bfloat16),
    }


def reference(features, project, bias, send_rows, send_count, block_ids, block_weights):
    width = F // N_FEAT
    total = jnp.zeros((NODES, HID), jnp.float32)
    for slice_index in range(N_FEAT):
        lo = slice_index * width
        partial_sum = jnp.dot(features[:, lo:lo + width], project[lo:lo + width, :], preferred_element_type=jnp.float32)
        rounded = lax.optimization_barrier(partial_sum.astype(jnp.bfloat16))
        total = total + rounded.astype(jnp.float32)
    projected = total.astype(jnp.bfloat16)
    owned = projected.reshape(N_BULK, N_FEAT, DST, HID).transpose(1, 0, 2, 3).reshape(DEVICES, DST, HID)
    slots = jnp.arange(CAP, dtype=jnp.int32)
    senders = jnp.arange(DEVICES, dtype=jnp.int32)

    def one_device(receiver):
        rows = send_rows[:, receiver, :]
        counts = send_count[:, receiver]
        got = owned[senders[:, None], rows]
        live = (slots[None, :] < counts[:, None])[:, :, None]
        got = jnp.where(live, got, jnp.zeros_like(got))
        buffer = jnp.concatenate([owned[receiver], got.reshape(DEVICES * CAP, HID)], axis=0)
        buffer = buffer.reshape(NBLK, BLK, HID)
        sources = buffer[block_ids[receiver]].astype(jnp.float32)
        weights = block_weights[receiver].astype(jnp.float32)
        summed = jnp.einsum("tkij,tkjh->tih", weights, sources)
        return jax.nn.relu(summed.reshape(DST, HID) + bias).astype(jnp.bfloat16)

    states = lax.map(one_device, jnp.arange(DEVICES, dtype=jnp.int32))
    return states.reshape(N_FEAT, N_BULK, DST, HID).transpose(1, 0, 2, 3).reshape(NODES, HID)
```

```python
import jax
import jax.numpy as jnp
from jax import lax
from jax.experimental import pallas as pl
from jax.experimental.pallas import tpu as pltpu
from jax.sharding import PartitionSpec as P

MESH = pl.DeviceIdType.MESH

SIDE = 4
OWN = 2048
HALF = OWN // 2
PIECE = 256
PER_HALF = HALF // PIECE
UNITS = 2 * SIDE * PER_HALF
STAGE = 2 * PER_HALF
LAG = 4
SLOTS = 4
CAP = 64
HID = 256
DEV = 128
GROUP = 4
BLK = 128
STEP = 23


def rem(a, n):
    return lax.rem(a, jnp.int32(n))


def div(a, n):
    return lax.div(a, jnp.int32(n))


def kernel(
    x_hbm, w_ref, bias_ref, rows_ref, count_ref, ids_ref, bw_hbm, out_ref,
    xbuf, own, sib_out, sib_in, ring_in, buf, outgoing, weights, picks,
    x_sem, sib_send, sib_recv, ring_send, ring_recv, out_send, out_recv, self_sem, w_sem, meet,
):
    feat = lax.axis_index("feat")
    bulk = lax.axis_index("bulk")
    z, c = div(feat, 2), rem(feat, 2)
    y, x = div(bulk, SIDE), rem(bulk, SIDE)
    me = feat * 16 + bulk

    def at(dx, dy, dz, dc):
        return (
            rem(z + dz, SIDE) * 2 + rem(c + dc, 2),
            rem(y + dy, SIDE) * SIDE + rem(x + dx, SIDE),
        )

    sibling = at(0, 0, 0, 1)
    axis_pairs = (
        (at(1, 0, 0, 0), at(3, 0, 0, 0)),
        (at(0, 1, 0, 0), at(0, 3, 0, 0)),
        (at(0, 0, 1, 0), at(0, 0, 3, 0)),
    )
    rounds = (axis_pairs[0], axis_pairs[1], axis_pairs[1], axis_pairs[2], axis_pairs[2], (sibling,))

    def unit_place(u):
        stage, j, side = div(u, STAGE), rem(div(u, 2), PER_HALF), rem(u, 2)
        dz = jnp.where(stage == 0, 2, jnp.where(stage == 3, 0, 1 + 2 * side))
        half = jnp.where(stage == 1, 1 - side, side)
        return rem(z + dz, SIDE), half * HALF + j * PIECE

    def fetch(u):
        block, row = unit_place(u)
        slot = rem(u, SLOTS)
        return pltpu.make_async_copy(
            x_hbm.at[pl.ds(block * 2, 2), pl.ds(row, PIECE), :], xbuf.at[slot], x_sem.at[slot]
        )

    for u in range(SLOTS - 1):
        fetch(jnp.int32(u)).start()
    load_weights = pltpu.make_async_copy(bw_hbm, weights, w_sem)
    load_weights.start()

    barrier = pltpu.get_barrier_semaphore()
    neighbours = [sibling] + [d for pair in axis_pairs for d in pair]
    for d in neighbours:
        pl.semaphore_signal(barrier, inc=1, device_id=d, device_id_type=MESH)
    picked = rows_ref[...].astype(jnp.float32)
    slot_of = lax.broadcasted_iota(jnp.int32, (CAP, DEV), 0)
    picks[...] = jnp.where(slot_of < count_ref[...], picked, -1.0)
    pl.semaphore_wait(barrier, len(neighbours))

    def greet(r):
        for d in rounds[r]:
            pl.semaphore_signal(meet.at[r], inc=1, device_id=d, device_id_type=MESH)

    def greeted(r):
        pl.semaphore_wait(meet.at[r], len(rounds[r]))

    greet(0)

    def piece(u):
        return pl.ds(pl.multiple_of(u * PIECE, PIECE), PIECE)

    def to_sibling(u):
        return pltpu.make_async_remote_copy(
            src_ref=sib_out.at[piece(u)], dst_ref=sib_in.at[piece(u)],
            send_sem=sib_send, recv_sem=sib_recv.at[u], device_id=sibling, device_id_type=MESH,
        )

    def along(u):
        target = at(0, 0, 1 + 2 * rem(u, 2), 0)
        return pltpu.make_async_remote_copy(
            src_ref=own.at[piece(u)], dst_ref=ring_in.at[piece(u)],
            send_sem=ring_send, recv_sem=ring_recv.at[u], device_id=target, device_id_type=MESH,
        )

    def reduce_step(u, _):
        @pl.when(u < UNITS)
        def _():
            @pl.when(u + (SLOTS - 1) < UNITS)
            def _():
                fetch(u + (SLOTS - 1)).start()

            slot = rem(u, SLOTS)
            fetch(u).wait()
            sib_out[piece(u), :] = jnp.dot(
                xbuf[slot, 1 - c], w_ref[...], preferred_element_type=jnp.float32
            ).astype(jnp.bfloat16)
            to_sibling(u).start()
            own[piece(u), :] = jnp.dot(
                xbuf[slot, c], w_ref[...], preferred_element_type=jnp.float32
            ).astype(jnp.bfloat16)

        for r in range(len(rounds) - 1):
            @pl.when(u == 6 + 5 * r)
            def _():
                greeted(r)
                greet(r + 1)

        v = u - LAG

        @pl.when(v >= 0)
        def _():
            to_sibling(v).wait_recv()
            own[piece(v), :] = (
                own[piece(v), :].astype(jnp.float32) + sib_in[piece(v), :].astype(jnp.float32)
            ).astype(jnp.bfloat16)

            @pl.when(v < 2 * STAGE)
            def _():
                along(v).start()

        return 0

    lax.fori_loop(0, UNITS + LAG, reduce_step, 0)

    def relay_step(i, _):
        along(i).wait_recv()
        v = 2 * STAGE + i
        own[piece(v), :] = (
            own[piece(v), :].astype(jnp.float32) + ring_in[piece(i), :].astype(jnp.float32)
        ).astype(jnp.bfloat16)
        along(v).start()
        return 0

    lax.fori_loop(0, STAGE, relay_step, 0)
    greeted(len(rounds) - 1)

    def finish_step(i, _):
        side = rem(i, 2)
        direct, relayed, mine = STAGE + i + 1 - 2 * side, 2 * STAGE + i, 3 * STAGE + i
        along(direct).wait_recv()
        along(relayed).wait_recv()
        total = (
            own[piece(mine), :].astype(jnp.float32)
            + ring_in[piece(direct), :].astype(jnp.float32)
            + ring_in[piece(relayed), :].astype(jnp.float32)
        )
        block = (side * HALF + div(i, 2) * PIECE) // BLK
        buf[pl.ds(block, PIECE // BLK)] = total.astype(jnp.bfloat16).reshape(PIECE // BLK, BLK, HID)
        return 0

    lax.fori_loop(0, STAGE, finish_step, 0)

    lane = lax.broadcasted_iota(jnp.int32, (CAP, DEV), 1)
    node = lax.broadcasted_iota(jnp.int32, (GROUP * CAP, PIECE), 1).astype(jnp.float32)
    landing = buf.at[OWN // BLK + div(me, 2), pl.ds(pl.multiple_of(rem(me, 2) * CAP, CAP), CAP)]

    def receiver(k):
        v = jnp.where(k < DEV - 1, 1 + rem(STEP * k, DEV - 1), 0)
        return at(rem(v, 4), rem(div(v, 4), 4), div(v, 32), rem(div(v, 16), 2))

    def send(k):
        return pltpu.make_async_remote_copy(
            src_ref=outgoing.at[pl.ds(pl.multiple_of(k * CAP, CAP), CAP)],
            dst_ref=landing,
            send_sem=out_send, recv_sem=out_recv, device_id=receiver(k), device_id_type=MESH,
        )

    def gather_step(g, _):
        columns = []
        for q in range(GROUP):
            to_feat, to_bulk = receiver(g * GROUP + q)
            chosen = lane == to_feat * 16 + to_bulk
            columns.append(jnp.sum(jnp.where(chosen, picks[...], 0.0), axis=1, keepdims=True))
        column = jnp.concatenate(columns, axis=0)
        rows = jnp.zeros((GROUP * CAP, HID), jnp.float32)
        for t in range(OWN // PIECE):
            hot = jnp.where(column - float(t * PIECE) == node, 1.0, 0.0).astype(jnp.bfloat16)
            rows += jnp.dot(
                hot, buf[2 * t:2 * t + 2].reshape(PIECE, HID), preferred_element_type=jnp.float32
            )
        start = pl.multiple_of(g * (GROUP * CAP), GROUP * CAP)
        outgoing[pl.ds(start, GROUP * CAP), :] = rows.astype(jnp.bfloat16)
        for q in range(GROUP - 1):
            send(g * GROUP + q).start()

        @pl.when(g < DEV // GROUP - 1)
        def _():
            send(g * GROUP + GROUP - 1).start()

        return 0

    lax.fori_loop(0, DEV // GROUP, gather_step, 0)
    last = pltpu.make_async_copy(
        outgoing.at[pl.ds((DEV - 1) * CAP, CAP)], landing, self_sem
    )
    last.start()
    last.wait()
    sent = outgoing.at[pl.ds(0, (DEV - 1) * CAP)]
    pltpu.make_async_copy(sent, sent, out_recv).wait()
    load_weights.wait()

    def tile_step(t, _):
        total = jnp.zeros((BLK, HID), jnp.float32)
        for k in range(0, 12, 2):
            blocks = [buf[ids_ref[k, t]], buf[ids_ref[k + 1, t]]]
            total += jnp.dot(
                jnp.concatenate([weights[t, k], weights[t, k + 1]], axis=1),
                jnp.concatenate(blocks, axis=0),
                preferred_element_type=jnp.float32,
            )
        row = pl.multiple_of(t * BLK, BLK)
        out_ref[pl.ds(row, BLK), :] = jnp.maximum(total + bias_ref[...], 0.0).astype(jnp.bfloat16)
        return 0

    lax.fori_loop(0, 16, tile_step, 0)

    pltpu.make_async_copy(sent, sent, out_send).wait()
    pltpu.make_async_copy(sib_out, sib_out, sib_send).wait()
    ringed = own.at[pl.ds(0, 3 * STAGE * PIECE)]
    pltpu.make_async_copy(ringed, ringed, ring_send).wait()


def per_device(features, project, bias, send_rows, send_count, block_ids, block_weights):
    vmem = pl.BlockSpec(memory_space=pltpu.VMEM)
    anywhere = pl.BlockSpec(memory_space=pl.ANY)
    bf16 = jnp.bfloat16
    return pl.pallas_call(
        kernel,
        out_shape=jax.ShapeDtypeStruct((OWN, HID), bf16),
        in_specs=[
            anywhere, vmem, vmem, vmem, vmem, pl.BlockSpec(memory_space=pltpu.SMEM), anywhere,
        ],
        out_specs=vmem,
        scratch_shapes=[
            pltpu.VMEM((SLOTS, 2, PIECE, 512), bf16),
            pltpu.VMEM((UNITS * PIECE, HID), bf16),
            pltpu.VMEM((UNITS * PIECE, HID), bf16),
            pltpu.VMEM((UNITS * PIECE, HID), bf16),
            pltpu.VMEM((3 * STAGE * PIECE, HID), bf16),
            pltpu.VMEM(((OWN + DEV * CAP) // BLK, BLK, HID), bf16),
            pltpu.VMEM((DEV * CAP, HID), bf16),
            pltpu.VMEM((16, 12, BLK, BLK), bf16),
            pltpu.VMEM((CAP, DEV), jnp.float32),
            pltpu.SemaphoreType.DMA((SLOTS,)),
            pltpu.SemaphoreType.DMA,
            pltpu.SemaphoreType.DMA((UNITS,)),
            pltpu.SemaphoreType.DMA,
            pltpu.SemaphoreType.DMA((3 * STAGE,)),
            pltpu.SemaphoreType.DMA,
            pltpu.SemaphoreType.DMA,
            pltpu.SemaphoreType.DMA,
            pltpu.SemaphoreType.DMA,
            pltpu.SemaphoreType.REGULAR((6,)),
        ],
        compiler_params=pltpu.CompilerParams(
            collective_id=0, has_side_effects=True, vmem_limit_bytes=56 * 1024 * 1024
        ),
        cost_estimate=pl.CostEstimate(
            flops=15_000_000_000, bytes_accessed=24 * 1024 * 1024, transcendentals=0
        ),
    )(
        features.reshape(8, OWN, 512), project, bias.reshape(1, HID), send_rows[0].T, send_count,
        block_ids[0].T, block_weights[0],
    )


def solution(mesh):
    placed = (
        P("bulk", "feat"),
        P("feat", None),
        P(),
        P(("feat", "bulk"), None, None),
        P(("feat", "bulk"), None),
        P(("feat", "bulk"), None, None),
        P(("feat", "bulk"), None, None, None, None),
    )
    return jax.shard_map(
        per_device, mesh=mesh, in_specs=placed, out_specs=P(("bulk", "feat"), None), check_vma=False
    )
```

```python
import jax
import jax.numpy as jnp
from jax import lax
from jax.experimental import pallas as pl
from jax.experimental.pallas import tpu as pltpu
from jax.sharding import PartitionSpec as P

MESH = pl.DeviceIdType.MESH

SIDE = 4
OWN = 2048
HALF = OWN // 2
PIECE = 256
PER_HALF = HALF // PIECE
UNITS = 2 * SIDE * PER_HALF
STAGE = 2 * PER_HALF
LAG = 3
EARLY = 3
SLOTS = 4
CAP = 64
HID = 256
DEV = 128
GROUP = 4
BLK = 128
TOGETHER = 4
STEP = 23


def rem(a, n):
    return lax.rem(a, jnp.int32(n))


def div(a, n):
    return lax.div(a, jnp.int32(n))


def kernel(
    x_hbm, w_ref, bias_ref, rows_ref, count_ref, ids_ref, bw_hbm, out_ref,
    xbuf, own, sib_out, sib_in, ring_in, buf, outgoing, weights, picks,
    x_sem, sib_send, sib_recv, ring_send, ring_recv, out_send, out_recv, self_sem, w_sem, meet,
):
    feat = lax.axis_index("feat")
    bulk = lax.axis_index("bulk")
    z, c = div(feat, 2), rem(feat, 2)
    y, x = div(bulk, SIDE), rem(bulk, SIDE)
    me = feat * 16 + bulk

    def at(dx, dy, dz, dc):
        return (
            rem(z + dz, SIDE) * 2 + rem(c + dc, 2),
            rem(y + dy, SIDE) * SIDE + rem(x + dx, SIDE),
        )

    sibling = at(0, 0, 0, 1)
    along_x = [at(d, 0, 0, 0) for d in range(1, SIDE)]
    along_y = [at(0, d, 0, 0) for d in range(1, SIDE)]
    along_z = [at(0, 0, d, 0) for d in range(1, SIDE)]
    rounds = (along_x, along_z, [sibling])

    def unit_place(u):
        stage, j, side = div(u, STAGE), rem(div(u, 2), PER_HALF), rem(u, 2)
        dz = jnp.where(stage == 0, 2, jnp.where(stage == 3, 0, 1 + 2 * side))
        half = jnp.where(stage == 1, 1 - side, side)
        return rem(z + dz, SIDE), half * HALF + j * PIECE

    def fetch(u):
        block, row = unit_place(u)
        slot = rem(u, SLOTS)
        return [
            pltpu.make_async_copy(
                x_hbm.at[block * 2 + e, pl.ds(row, PIECE), :], xbuf.at[slot, i], x_sem.at[slot]
            )
            for i, e in enumerate((c, 1 - c))
        ]

    for u in range(SLOTS - 1):
        for f in fetch(jnp.int32(u)):
            f.start()
    load_weights = pltpu.make_async_copy(bw_hbm, weights, w_sem)

    barrier = pltpu.get_barrier_semaphore()
    neighbours = [sibling] + along_x + along_y + along_z
    for d in neighbours:
        pl.semaphore_signal(barrier, inc=1, device_id=d, device_id_type=MESH)
    picked = rows_ref[...].astype(jnp.float32)
    slot_of = lax.broadcasted_iota(jnp.int32, (CAP, DEV), 0)
    picks[...] = jnp.where(slot_of < count_ref[...], picked, -1.0)

    def greet(r):
        for d in rounds[r]:
            pl.semaphore_signal(meet.at[r], inc=1, device_id=d, device_id_type=MESH)

    def greeted(r):
        pl.semaphore_wait(meet.at[r], len(rounds[r]))

    def piece(u):
        return pl.ds(pl.multiple_of(u * PIECE, PIECE), PIECE)

    def to_sibling(u):
        return pltpu.make_async_remote_copy(
            src_ref=sib_out.at[piece(u)], dst_ref=sib_in.at[piece(u)],
            send_sem=sib_send, recv_sem=sib_recv.at[u], device_id=sibling, device_id_type=MESH,
        )

    def along(u):
        target = at(0, 0, 1 + 2 * rem(u, 2), 0)
        return pltpu.make_async_remote_copy(
            src_ref=own.at[piece(u)], dst_ref=ring_in.at[piece(u)],
            send_sem=ring_send, recv_sem=ring_recv.at[u], device_id=target, device_id_type=MESH,
        )

    def product(u):
        @pl.when(u + (SLOTS - 1) < UNITS)
        def _():
            for f in fetch(u + (SLOTS - 1)):
                f.start()

        slot = rem(u, SLOTS)
        pltpu.make_async_copy(xbuf.at[slot], xbuf.at[slot], x_sem.at[slot]).wait()
        both = jnp.dot(
            xbuf[slot].reshape(2 * PIECE, 512), w_ref[...], preferred_element_type=jnp.float32
        ).astype(jnp.bfloat16)
        sib_out[piece(u), :] = both[PIECE:]
        own[piece(u), :] = both[:PIECE]

    def early_step(u, _):
        product(u)
        return 0

    lax.fori_loop(0, EARLY, early_step, 0)
    pl.semaphore_wait(barrier, len(neighbours))
    for u in range(EARLY):
        to_sibling(jnp.int32(u)).start()
    greet(0)
    load_weights.start()

    def reduce_step(u, _):
        @pl.when(u < UNITS)
        def _():
            product(u)
            to_sibling(u).start()

        for r in range(len(rounds) - 1):
            @pl.when(u == 12 + 8 * r)
            def _():
                greeted(r)
                greet(r + 1)

        v = u - LAG

        @pl.when(v >= 0)
        def _():
            to_sibling(v).wait_recv()
            own[piece(v), :] = (
                own[piece(v), :].astype(jnp.float32) + sib_in[piece(v), :].astype(jnp.float32)
            ).astype(jnp.bfloat16)

            @pl.when(v < 2 * STAGE)
            def _():
                along(v).start()

        return 0

    lax.fori_loop(EARLY, UNITS + LAG, reduce_step, 0)

    def relay_step(i, _):
        along(i).wait_recv()
        v = 2 * STAGE + i
        own[piece(v), :] = (
            own[piece(v), :].astype(jnp.float32) + ring_in[piece(i), :].astype(jnp.float32)
        ).astype(jnp.bfloat16)
        along(v).start()
        return 0

    lax.fori_loop(0, STAGE, relay_step, 0)
    greeted(len(rounds) - 1)

    def finish_step(i, _):
        side = rem(i, 2)
        direct, relayed, mine = STAGE + i + 1 - 2 * side, 2 * STAGE + i, 3 * STAGE + i
        along(direct).wait_recv()
        along(relayed).wait_recv()
        total = (
            own[piece(mine), :].astype(jnp.float32)
            + ring_in[piece(direct), :].astype(jnp.float32)
            + ring_in[piece(relayed), :].astype(jnp.float32)
        )
        block = (side * HALF + div(i, 2) * PIECE) // BLK
        buf[pl.ds(block, PIECE // BLK)] = total.astype(jnp.bfloat16).reshape(PIECE // BLK, BLK, HID)
        return 0

    lax.fori_loop(0, STAGE, finish_step, 0)

    lane = lax.broadcasted_iota(jnp.int32, (CAP, DEV), 1)
    node = lax.broadcasted_iota(jnp.int32, (GROUP * CAP, PIECE), 1).astype(jnp.bfloat16)
    landing = buf.at[OWN // BLK + div(me, 2), pl.ds(pl.multiple_of(rem(me, 2) * CAP, CAP), CAP)]

    def receiver(k):
        v = jnp.where(k < DEV - 1, 1 + rem(STEP * k, DEV - 1), 0)
        return at(rem(v, 4), rem(div(v, 4), 4), div(v, 32), rem(div(v, 16), 2))

    def send(k):
        return pltpu.make_async_remote_copy(
            src_ref=outgoing.at[pl.ds(pl.multiple_of(k * CAP, CAP), CAP)],
            dst_ref=landing,
            send_sem=out_send, recv_sem=out_recv, device_id=receiver(k), device_id_type=MESH,
        )

    def gather_step(g, _):
        columns = []
        for q in range(GROUP):
            to_feat, to_bulk = receiver(g * GROUP + q)
            chosen = lane == to_feat * 16 + to_bulk
            columns.append(jnp.sum(jnp.where(chosen, picks[...], 0.0), axis=1, keepdims=True))
        column = jnp.concatenate(columns, axis=0)
        rows = jnp.zeros((GROUP * CAP, HID), jnp.float32)
        for t in range(OWN // PIECE):
            near = column - float(t * PIECE)
            near = jnp.where((near >= 0.0) & (near < float(PIECE)), near, -1.0).astype(jnp.bfloat16)
            hot = jnp.where(near == node, jnp.bfloat16(1), jnp.bfloat16(0))
            rows += jnp.dot(
                hot, buf[2 * t:2 * t + 2].reshape(PIECE, HID), preferred_element_type=jnp.float32
            )
        start = pl.multiple_of(g * (GROUP * CAP), GROUP * CAP)
        outgoing[pl.ds(start, GROUP * CAP), :] = rows.astype(jnp.bfloat16)
        for q in range(GROUP - 1):
            send(g * GROUP + q).start()

        @pl.when(g < DEV // GROUP - 1)
        def _():
            send(g * GROUP + GROUP - 1).start()

        return 0

    lax.fori_loop(0, DEV // GROUP, gather_step, 0)
    last = pltpu.make_async_copy(
        outgoing.at[pl.ds((DEV - 1) * CAP, CAP)], landing, self_sem
    )
    last.start()
    last.wait()
    sent = outgoing.at[pl.ds(0, (DEV - 1) * CAP)]
    pltpu.make_async_copy(sent, sent, out_recv).wait()
    load_weights.wait()

    def tile_step(i, _):
        for e in range(TOGETHER):
            t = i * TOGETHER + e
            total = jnp.zeros((BLK, HID), jnp.float32)
            for k in range(0, 12, 2):
                blocks = [buf[ids_ref[k, 0, t]], buf[ids_ref[k + 1, 0, t]]]
                total += jnp.dot(
                    jnp.concatenate([weights[t, k], weights[t, k + 1]], axis=1),
                    jnp.concatenate(blocks, axis=0),
                    preferred_element_type=jnp.float32,
                )
            row = pl.multiple_of(t * BLK, BLK)
            out_ref[pl.ds(row, BLK), :] = (total + bias_ref[...]).astype(jnp.bfloat16)
        return 0

    lax.fori_loop(0, 16 // TOGETHER, tile_step, 0)

    pltpu.make_async_copy(sent, sent, out_send).wait()
    pltpu.make_async_copy(sib_out, sib_out, sib_send).wait()
    ringed = own.at[pl.ds(0, 3 * STAGE * PIECE)]
    pltpu.make_async_copy(ringed, ringed, ring_send).wait()


def per_device(features, project, bias, send_rows, send_count, block_ids, block_weights):
    vmem = pl.BlockSpec(memory_space=pltpu.VMEM)
    anywhere = pl.BlockSpec(memory_space=pl.ANY)
    bf16 = jnp.bfloat16
    summed = pl.pallas_call(
        kernel,
        out_shape=jax.ShapeDtypeStruct((OWN, HID), bf16),
        in_specs=[
            anywhere, vmem, vmem, vmem, vmem, pl.BlockSpec(memory_space=pltpu.SMEM), anywhere,
        ],
        out_specs=vmem,
        scratch_shapes=[
            pltpu.VMEM((SLOTS, 2, PIECE, 512), bf16),
            pltpu.VMEM((UNITS * PIECE, HID), bf16),
            pltpu.VMEM((UNITS * PIECE, HID), bf16),
            pltpu.VMEM((UNITS * PIECE, HID), bf16),
            pltpu.VMEM((3 * STAGE * PIECE, HID), bf16),
            pltpu.VMEM(((OWN + DEV * CAP) // BLK, BLK, HID), bf16),
            pltpu.VMEM((DEV * CAP, HID), bf16),
            pltpu.VMEM((16, 12, BLK, BLK), bf16),
            pltpu.VMEM((CAP, DEV), jnp.float32),
            pltpu.SemaphoreType.DMA((SLOTS,)),
            pltpu.SemaphoreType.DMA,
            pltpu.SemaphoreType.DMA((UNITS,)),
            pltpu.SemaphoreType.DMA,
            pltpu.SemaphoreType.DMA((3 * STAGE,)),
            pltpu.SemaphoreType.DMA,
            pltpu.SemaphoreType.DMA,
            pltpu.SemaphoreType.DMA,
            pltpu.SemaphoreType.DMA,
            pltpu.SemaphoreType.REGULAR((3,)),
        ],
        compiler_params=pltpu.CompilerParams(
            collective_id=0, has_side_effects=True, vmem_limit_bytes=56 * 1024 * 1024
        ),
        cost_estimate=pl.CostEstimate(
            flops=15_000_000_000, bytes_accessed=24 * 1024 * 1024, transcendentals=0
        ),
    )(
        features.reshape(8, OWN, 512), project, bias.reshape(1, HID), send_rows[0].T, send_count,
        block_ids.transpose(2, 0, 1), block_weights[0],
    )
    return jnp.maximum(summed, 0)


def solution(mesh):
    placed = (
        P("bulk", "feat"),
        P("feat", None),
        P(),
        P(("feat", "bulk"), None, None),
        P(("feat", "bulk"), None),
        P(("feat", "bulk"), None, None),
        P(("feat", "bulk"), None, None, None, None),
    )
    return jax.shard_map(
        per_device, mesh=mesh, in_specs=placed, out_specs=P(("bulk", "feat"), None), check_vma=False
    )
```

```python
import jax
import jax.numpy as jnp
from jax import lax
from jax.experimental import pallas as pl
from jax.experimental.pallas import tpu as pltpu
from jax.sharding import PartitionSpec as P

MESH = pl.DeviceIdType.MESH

SIDE = 4
OWN = 2048
HALF = OWN // 2
PIECE = 256
PER_HALF = HALF // PIECE
UNITS = 2 * SIDE * PER_HALF
STAGE = 2 * PER_HALF
LAG = 2
EARLY = 2
SLOTS = 4
CAP = 64
HID = 256
DEV = 128
GROUP = 4
BLK = 128
TOGETHER = 8
STEP = 23


def rem(a, n):
    return lax.rem(a, jnp.int32(n))


def div(a, n):
    return lax.div(a, jnp.int32(n))


def kernel(
    x_hbm, w_ref, bias_ref, rows_ref, count_ref, ids_ref, bw_hbm, out_ref,
    xbuf, own, sib_out, sib_in, ring_in, buf, outgoing, weights, picks,
    x_sem, sib_send, sib_recv, ring_send, ring_recv, out_send, out_recv, self_sem, w_sem, meet,
):
    feat = lax.axis_index("feat")
    bulk = lax.axis_index("bulk")
    z, c = div(feat, 2), rem(feat, 2)
    y, x = div(bulk, SIDE), rem(bulk, SIDE)
    me = feat * 16 + bulk

    def at(dx, dy, dz, dc):
        return (
            rem(z + dz, SIDE) * 2 + rem(c + dc, 2),
            rem(y + dy, SIDE) * SIDE + rem(x + dx, SIDE),
        )

    sibling = at(0, 0, 0, 1)
    along_x = [at(d, 0, 0, 0) for d in range(1, SIDE)]
    along_y = [at(0, d, 0, 0) for d in range(1, SIDE)]
    along_z = [at(0, 0, d, 0) for d in range(1, SIDE)]
    rounds = (along_x, along_z, [sibling])

    def unit_place(u):
        stage, j, side = div(u, STAGE), rem(div(u, 2), PER_HALF), rem(u, 2)
        dz = jnp.where(stage == 0, 2, jnp.where(stage == 3, 0, 1 + 2 * side))
        half = jnp.where(stage == 1, 1 - side, side)
        return rem(z + dz, SIDE), half * HALF + j * PIECE

    def fetch(u):
        block, row = unit_place(u)
        slot = rem(u, SLOTS)
        return [
            pltpu.make_async_copy(
                x_hbm.at[block * 2 + e, pl.ds(row, PIECE), :], xbuf.at[slot, i], x_sem.at[slot]
            )
            for i, e in enumerate((c, 1 - c))
        ]

    for u in range(SLOTS - 1):
        for f in fetch(jnp.int32(u)):
            f.start()
    load_weights = pltpu.make_async_copy(bw_hbm, weights, w_sem)

    barrier = pltpu.get_barrier_semaphore()
    neighbours = [sibling] + along_x + along_y + along_z
    for d in neighbours:
        pl.semaphore_signal(barrier, inc=1, device_id=d, device_id_type=MESH)
    picked = rows_ref[...].astype(jnp.float32)
    slot_of = lax.broadcasted_iota(jnp.int32, (CAP, DEV), 0)
    picks[...] = jnp.where(slot_of < count_ref[...], picked, -1.0)

    def greet(r):
        for d in rounds[r]:
            pl.semaphore_signal(meet.at[r], inc=1, device_id=d, device_id_type=MESH)

    def greeted(r):
        pl.semaphore_wait(meet.at[r], len(rounds[r]))

    def piece(u):
        return pl.ds(pl.multiple_of(u * PIECE, PIECE), PIECE)

    def to_sibling(u):
        return pltpu.make_async_remote_copy(
            src_ref=sib_out.at[piece(u)], dst_ref=sib_in.at[piece(u)],
            send_sem=sib_send, recv_sem=sib_recv.at[u], device_id=sibling, device_id_type=MESH,
        )

    def along(u):
        target = at(0, 0, 1 + 2 * rem(u, 2), 0)
        return pltpu.make_async_remote_copy(
            src_ref=own.at[piece(u)], dst_ref=ring_in.at[piece(u)],
            send_sem=ring_send, recv_sem=ring_recv.at[u], device_id=target, device_id_type=MESH,
        )

    def product(u):
        @pl.when(u + (SLOTS - 1) < UNITS)
        def _():
            for f in fetch(u + (SLOTS - 1)):
                f.start()

        slot = rem(u, SLOTS)
        pltpu.make_async_copy(xbuf.at[slot], xbuf.at[slot], x_sem.at[slot]).wait()
        both = jnp.dot(
            xbuf[slot].reshape(2 * PIECE, 512), w_ref[...], preferred_element_type=jnp.float32
        ).astype(jnp.bfloat16)
        sib_out[piece(u), :] = both[PIECE:]
        own[piece(u), :] = both[:PIECE]

    def early_step(u, _):
        product(u)
        return 0

    lax.fori_loop(0, EARLY, early_step, 0)
    pl.semaphore_wait(barrier, len(neighbours))
    for u in range(EARLY):
        to_sibling(jnp.int32(u)).start()
    greet(0)
    load_weights.start()

    def reduce_step(u, _):
        @pl.when(u < UNITS)
        def _():
            product(u)
            to_sibling(u).start()

        for r in range(len(rounds) - 1):
            @pl.when(u == 12 + 8 * r)
            def _():
                greeted(r)
                greet(r + 1)

        v = u - LAG

        @pl.when(v >= 0)
        def _():
            to_sibling(v).wait_recv()
            own[piece(v), :] = (
                own[piece(v), :].astype(jnp.float32) + sib_in[piece(v), :].astype(jnp.float32)
            ).astype(jnp.bfloat16)

            @pl.when(v < 2 * STAGE)
            def _():
                along(v).start()

        return 0

    lax.fori_loop(EARLY, UNITS + LAG, reduce_step, 0)

    def relay_step(i, _):
        along(i).wait_recv()
        v = 2 * STAGE + i
        own[piece(v), :] = (
            own[piece(v), :].astype(jnp.float32) + ring_in[piece(i), :].astype(jnp.float32)
        ).astype(jnp.bfloat16)
        along(v).start()
        return 0

    lax.fori_loop(0, STAGE, relay_step, 0)
    greeted(len(rounds) - 1)

    def finish_step(i, _):
        side = rem(i, 2)
        direct, relayed, mine = STAGE + i + 1 - 2 * side, 2 * STAGE + i, 3 * STAGE + i
        along(direct).wait_recv()
        along(relayed).wait_recv()
        total = (
            own[piece(mine), :].astype(jnp.float32)
            + ring_in[piece(direct), :].astype(jnp.float32)
            + ring_in[piece(relayed), :].astype(jnp.float32)
        )
        block = (side * HALF + div(i, 2) * PIECE) // BLK
        buf[pl.ds(block, PIECE // BLK)] = total.astype(jnp.bfloat16).reshape(PIECE // BLK, BLK, HID)
        return 0

    lax.fori_loop(0, STAGE, finish_step, 0)

    lane = lax.broadcasted_iota(jnp.int32, (CAP, DEV), 1)
    node = lax.broadcasted_iota(jnp.int32, (GROUP * CAP, PIECE), 1).astype(jnp.bfloat16)
    landing = buf.at[OWN // BLK + div(me, 2), pl.ds(pl.multiple_of(rem(me, 2) * CAP, CAP), CAP)]

    def receiver(k):
        v = jnp.where(k < DEV - 1, 1 + rem(STEP * k, DEV - 1), 0)
        return at(rem(v, 4), rem(div(v, 4), 4), div(v, 32), rem(div(v, 16), 2))

    def send(k):
        return pltpu.make_async_remote_copy(
            src_ref=outgoing.at[pl.ds(pl.multiple_of(k * CAP, CAP), CAP)],
            dst_ref=landing,
            send_sem=out_send, recv_sem=out_recv, device_id=receiver(k), device_id_type=MESH,
        )

    def gather_step(g, _):
        columns = []
        for q in range(GROUP):
            to_feat, to_bulk = receiver(g * GROUP + q)
            chosen = lane == to_feat * 16 + to_bulk
            columns.append(jnp.sum(jnp.where(chosen, picks[...], 0.0), axis=1, keepdims=True))
        column = jnp.concatenate(columns, axis=0)
        rows = jnp.zeros((GROUP * CAP, HID), jnp.float32)
        for t in range(OWN // PIECE):
            near = column - float(t * PIECE)
            near = jnp.where((near >= 0.0) & (near < float(PIECE)), near, -1.0).astype(jnp.bfloat16)
            hot = jnp.where(near == node, jnp.bfloat16(1), jnp.bfloat16(0))
            rows += jnp.dot(
                hot, buf[2 * t:2 * t + 2].reshape(PIECE, HID), preferred_element_type=jnp.float32
            )
        start = pl.multiple_of(g * (GROUP * CAP), GROUP * CAP)
        outgoing[pl.ds(start, GROUP * CAP), :] = rows.astype(jnp.bfloat16)
        for q in range(GROUP - 1):
            send(g * GROUP + q).start()

        @pl.when(g < DEV // GROUP - 1)
        def _():
            send(g * GROUP + GROUP - 1).start()

        return 0

    lax.fori_loop(0, DEV // GROUP, gather_step, 0)
    last = pltpu.make_async_copy(
        outgoing.at[pl.ds((DEV - 1) * CAP, CAP)], landing, self_sem
    )
    last.start()
    last.wait()
    sent = outgoing.at[pl.ds(0, (DEV - 1) * CAP)]
    pltpu.make_async_copy(sent, sent, out_recv).wait()
    load_weights.wait()

    def tile_step(i, _):
        for e in range(TOGETHER):
            t = i * TOGETHER + e
            total = jnp.zeros((BLK, HID), jnp.float32)
            for k in range(0, 12, 2):
                blocks = [buf[ids_ref[k, 0, t]], buf[ids_ref[k + 1, 0, t]]]
                total += jnp.dot(
                    jnp.concatenate([weights[t, k], weights[t, k + 1]], axis=1),
                    jnp.concatenate(blocks, axis=0),
                    preferred_element_type=jnp.float32,
                )
            row = pl.multiple_of(t * BLK, BLK)
            out_ref[pl.ds(row, BLK), :] = (total + bias_ref[...]).astype(jnp.bfloat16)
        return 0

    lax.fori_loop(0, 16 // TOGETHER, tile_step, 0)

    pltpu.make_async_copy(sent, sent, out_send).wait()
    pltpu.make_async_copy(sib_out, sib_out, sib_send).wait()
    ringed = own.at[pl.ds(0, 3 * STAGE * PIECE)]
    pltpu.make_async_copy(ringed, ringed, ring_send).wait()


def per_device(features, project, bias, send_rows, send_count, block_ids, block_weights):
    vmem = pl.BlockSpec(memory_space=pltpu.VMEM)
    anywhere = pl.BlockSpec(memory_space=pl.ANY)
    bf16 = jnp.bfloat16
    summed = pl.pallas_call(
        kernel,
        out_shape=jax.ShapeDtypeStruct((OWN, HID), bf16),
        in_specs=[
            anywhere, vmem, vmem, vmem, vmem, pl.BlockSpec(memory_space=pltpu.SMEM), anywhere,
        ],
        out_specs=vmem,
        scratch_shapes=[
            pltpu.VMEM((SLOTS, 2, PIECE, 512), bf16),
            pltpu.VMEM((UNITS * PIECE, HID), bf16),
            pltpu.VMEM((UNITS * PIECE, HID), bf16),
            pltpu.VMEM((UNITS * PIECE, HID), bf16),
            pltpu.VMEM((3 * STAGE * PIECE, HID), bf16),
            pltpu.VMEM(((OWN + DEV * CAP) // BLK, BLK, HID), bf16),
            pltpu.VMEM((DEV * CAP, HID), bf16),
            pltpu.VMEM((16, 12, BLK, BLK), bf16),
            pltpu.VMEM((CAP, DEV), jnp.float32),
            pltpu.SemaphoreType.DMA((SLOTS,)),
            pltpu.SemaphoreType.DMA,
            pltpu.SemaphoreType.DMA((UNITS,)),
            pltpu.SemaphoreType.DMA,
            pltpu.SemaphoreType.DMA((3 * STAGE,)),
            pltpu.SemaphoreType.DMA,
            pltpu.SemaphoreType.DMA,
            pltpu.SemaphoreType.DMA,
            pltpu.SemaphoreType.DMA,
            pltpu.SemaphoreType.REGULAR((3,)),
        ],
        compiler_params=pltpu.CompilerParams(
            collective_id=0, has_side_effects=True, vmem_limit_bytes=50 * 1024 * 1024
        ),
        cost_estimate=pl.CostEstimate(
            flops=15_000_000_000, bytes_accessed=24 * 1024 * 1024, transcendentals=0
        ),
    )(
        features.reshape(8, OWN, 512), project, bias.reshape(1, HID), send_rows[0].T, send_count,
        block_ids.transpose(2, 0, 1), block_weights[0],
    )
    return jnp.maximum(summed, 0)


def solution(mesh):
    placed = (
        P("bulk", "feat"),
        P("feat", None),
        P(),
        P(("feat", "bulk"), None, None),
        P(("feat", "bulk"), None),
        P(("feat", "bulk"), None, None),
        P(("feat", "bulk"), None, None, None, None),
    )
    return jax.shard_map(
        per_device, mesh=mesh, in_specs=placed, out_specs=P(("bulk", "feat"), None), check_vma=False
    )
```

```python
import jax
import jax.numpy as jnp
from jax import lax
from jax.experimental import pallas as pl
from jax.experimental.pallas import tpu as pltpu
from jax.sharding import PartitionSpec as P

MESH = pl.DeviceIdType.MESH

SIDE = 4
OWN = 2048
HALF = OWN // 2
PIECE = 256
PER_HALF = HALF // PIECE
UNITS = 2 * SIDE * PER_HALF
STAGE = 2 * PER_HALF
LAG = 2
EARLY = 2
SLOTS = 4
CAP = 64
HID = 256
DEV = 128
GROUP = 4
BLK = 128
TOGETHER = 8
STEP = 23


def rem(a, n):
    return lax.rem(a, jnp.int32(n))


def div(a, n):
    return lax.div(a, jnp.int32(n))


def kernel(
    x_hbm, w_ref, bias_ref, rows_ref, count_ref, ids_ref, bw_hbm, out_ref,
    xbuf, own, sib_out, sib_in, ring_in, buf, outgoing, weights, picks,
    x_sem, sib_send, sib_recv, ring_send, ring_recv, out_send, out_recv, self_sem, w_sem, meet,
):
    feat = lax.axis_index("feat")
    bulk = lax.axis_index("bulk")
    z, c = div(feat, 2), rem(feat, 2)
    y, x = div(bulk, SIDE), rem(bulk, SIDE)
    me = feat * 16 + bulk

    def at(dx, dy, dz, dc):
        return (
            rem(z + dz, SIDE) * 2 + rem(c + dc, 2),
            rem(y + dy, SIDE) * SIDE + rem(x + dx, SIDE),
        )

    sibling = at(0, 0, 0, 1)
    along_x = [at(d, 0, 0, 0) for d in range(1, SIDE)]
    along_y = [at(0, d, 0, 0) for d in range(1, SIDE)]
    along_z = [at(0, 0, d, 0) for d in range(1, SIDE)]
    rounds = (along_x, along_z, [sibling])

    def unit_place(u):
        stage, j, side = div(u, STAGE), rem(div(u, 2), PER_HALF), rem(u, 2)
        dz = jnp.where(stage == 0, 2, jnp.where(stage == 3, 0, 1 + 2 * side))
        half = jnp.where(stage == 1, 1 - side, side)
        return rem(z + dz, SIDE), half * HALF + j * PIECE

    def fetch(u):
        block, row = unit_place(u)
        slot = rem(u, SLOTS)
        return [
            pltpu.make_async_copy(
                x_hbm.at[block * 2 + e, pl.ds(row, PIECE), :], xbuf.at[slot, i], x_sem.at[slot]
            )
            for i, e in enumerate((c, 1 - c))
        ]

    for u in range(SLOTS - 1):
        for f in fetch(jnp.int32(u)):
            f.start()
    load_weights = pltpu.make_async_copy(bw_hbm, weights, w_sem)

    barrier = pltpu.get_barrier_semaphore()
    neighbours = [sibling] + along_x + along_y + along_z
    for d in neighbours:
        pl.semaphore_signal(barrier, inc=1, device_id=d, device_id_type=MESH)
    picked = rows_ref[...].astype(jnp.float32)
    slot_of = lax.broadcasted_iota(jnp.int32, (CAP, DEV), 0)
    picks[...] = jnp.where(slot_of < count_ref[...], picked, -1.0)

    def greet(r):
        for d in rounds[r]:
            pl.semaphore_signal(meet.at[r], inc=1, device_id=d, device_id_type=MESH)

    def greeted(r):
        pl.semaphore_wait(meet.at[r], len(rounds[r]))

    def piece(u):
        return pl.ds(pl.multiple_of(u * PIECE, PIECE), PIECE)

    def to_sibling(u):
        return pltpu.make_async_remote_copy(
            src_ref=sib_out.at[piece(u)], dst_ref=sib_in.at[piece(u)],
            send_sem=sib_send, recv_sem=sib_recv.at[u], device_id=sibling, device_id_type=MESH,
        )

    def along(u):
        target = at(0, 0, 1 + 2 * rem(u, 2), 0)
        return pltpu.make_async_remote_copy(
            src_ref=own.at[piece(u)], dst_ref=ring_in.at[piece(u)],
            send_sem=ring_send, recv_sem=ring_recv.at[u], device_id=target, device_id_type=MESH,
        )

    def product(u):
        @pl.when(u + (SLOTS - 1) < UNITS)
        def _():
            for f in fetch(u + (SLOTS - 1)):
                f.start()

        slot = rem(u, SLOTS)
        pltpu.make_async_copy(xbuf.at[slot], xbuf.at[slot], x_sem.at[slot]).wait()
        both = jnp.dot(
            xbuf[slot].reshape(2 * PIECE, 512), w_ref[...], preferred_element_type=jnp.float32
        ).astype(jnp.bfloat16)
        sib_out[piece(u), :] = both[PIECE:]
        own[piece(u), :] = both[:PIECE]

    def early_step(u, _):
        product(u)
        return 0

    lax.fori_loop(0, EARLY, early_step, 0)
    pl.semaphore_wait(barrier, len(neighbours))
    for u in range(EARLY):
        to_sibling(jnp.int32(u)).start()
    greet(0)
    load_weights.start()

    def reduce_step(u, _):
        @pl.when(u < UNITS)
        def _():
            product(u)
            to_sibling(u).start()

        for r in range(len(rounds) - 1):
            @pl.when(u == 12 + 8 * r)
            def _():
                greeted(r)
                greet(r + 1)

        v = u - LAG

        @pl.when(v >= 0)
        def _():
            to_sibling(v).wait_recv()
            own[piece(v), :] = (
                own[piece(v), :].astype(jnp.float32) + sib_in[piece(v), :].astype(jnp.float32)
            ).astype(jnp.bfloat16)

            @pl.when(v < 2 * STAGE)
            def _():
                along(v).start()

        return 0

    lax.fori_loop(EARLY, UNITS + LAG, reduce_step, 0)

    def relay_step(i, _):
        along(i).wait_recv()
        v = 2 * STAGE + i
        own[piece(v), :] = (
            own[piece(v), :].astype(jnp.float32) + ring_in[piece(i), :].astype(jnp.float32)
        ).astype(jnp.bfloat16)
        along(v).start()
        return 0

    lax.fori_loop(0, STAGE, relay_step, 0)
    greeted(len(rounds) - 1)

    def finish_step(i, _):
        side = rem(i, 2)
        direct, relayed, mine = STAGE + i + 1 - 2 * side, 2 * STAGE + i, 3 * STAGE + i
        along(direct).wait_recv()
        along(relayed).wait_recv()
        total = (
            own[piece(mine), :].astype(jnp.float32)
            + ring_in[piece(direct), :].astype(jnp.float32)
            + ring_in[piece(relayed), :].astype(jnp.float32)
        )
        block = (side * HALF + div(i, 2) * PIECE) // BLK
        buf[pl.ds(block, PIECE // BLK)] = total.astype(jnp.bfloat16).reshape(PIECE // BLK, BLK, HID)
        return 0

    lax.fori_loop(0, STAGE, finish_step, 0)

    lane = lax.broadcasted_iota(jnp.int32, (CAP, DEV), 1)
    node = lax.broadcasted_iota(jnp.int32, (GROUP * CAP, PIECE), 1).astype(jnp.bfloat16)
    landing = buf.at[OWN // BLK + div(me, 2), pl.ds(pl.multiple_of(rem(me, 2) * CAP, CAP), CAP)]

    def receiver(k):
        v = jnp.where(k < DEV - 1, 1 + rem(STEP * k, DEV - 1), 0)
        return at(rem(v, 4), rem(div(v, 4), 4), div(v, 32), rem(div(v, 16), 2))

    def send(k):
        return pltpu.make_async_remote_copy(
            src_ref=outgoing.at[pl.ds(pl.multiple_of(k * CAP, CAP), CAP)],
            dst_ref=landing,
            send_sem=out_send, recv_sem=out_recv, device_id=receiver(k), device_id_type=MESH,
        )

    def gather_step(g, _):
        columns = []
        for q in range(GROUP):
            to_feat, to_bulk = receiver(g * GROUP + q)
            chosen = lane == to_feat * 16 + to_bulk
            columns.append(jnp.sum(jnp.where(chosen, picks[...], 0.0), axis=1, keepdims=True))
        column = jnp.concatenate(columns, axis=0)
        rows = jnp.zeros((GROUP * CAP, HID), jnp.float32)
        for t in range(OWN // PIECE):
            near = column - float(t * PIECE)
            near = jnp.where((near >= 0.0) & (near < float(PIECE)), near, -1.0).astype(jnp.bfloat16)
            hot = jnp.where(near == node, jnp.bfloat16(1), jnp.bfloat16(0))
            rows += jnp.dot(
                hot, buf[2 * t:2 * t + 2].reshape(PIECE, HID), preferred_element_type=jnp.float32
            )
        start = pl.multiple_of(g * (GROUP * CAP), GROUP * CAP)
        outgoing[pl.ds(start, GROUP * CAP), :] = rows.astype(jnp.bfloat16)
        for q in range(GROUP - 1):
            send(g * GROUP + q).start()

        @pl.when(g < DEV // GROUP - 1)
        def _():
            send(g * GROUP + GROUP - 1).start()

        return 0

    lax.fori_loop(0, DEV // GROUP, gather_step, 0)
    last = pltpu.make_async_copy(
        outgoing.at[pl.ds((DEV - 1) * CAP, CAP)], landing, self_sem
    )
    last.start()
    last.wait()
    sent = outgoing.at[pl.ds(0, (DEV - 1) * CAP)]
    pltpu.make_async_copy(sent, sent, out_recv).wait()
    load_weights.wait()

    def tile_step(i, _):
        for e in range(TOGETHER):
            t = i * TOGETHER + e
            total = jnp.zeros((BLK, HID), jnp.float32)
            for k in range(0, 12, 2):
                blocks = [buf[ids_ref[k, 0, t]], buf[ids_ref[k + 1, 0, t]]]
                total += jnp.dot(
                    jnp.concatenate([weights[t, k], weights[t, k + 1]], axis=1),
                    jnp.concatenate(blocks, axis=0),
                    preferred_element_type=jnp.float32,
                )
            row = pl.multiple_of(t * BLK, BLK)
            out_ref[pl.ds(row, BLK), :] = (total + bias_ref[...]).astype(jnp.bfloat16)
        return 0

    lax.fori_loop(0, 16 // TOGETHER, tile_step, 0)

    pltpu.make_async_copy(sent, sent, out_send).wait()
    pltpu.make_async_copy(sib_out, sib_out, sib_send).wait()
    ringed = own.at[pl.ds(0, 3 * STAGE * PIECE)]
    pltpu.make_async_copy(ringed, ringed, ring_send).wait()


def per_device(features, project, bias, send_rows, send_count, block_ids, block_weights):
    vmem = pl.BlockSpec(memory_space=pltpu.VMEM)
    anywhere = pl.BlockSpec(memory_space=pl.ANY)
    bf16 = jnp.bfloat16
    summed = pl.pallas_call(
        kernel,
        out_shape=jax.ShapeDtypeStruct((OWN, HID), bf16),
        in_specs=[
            anywhere, vmem, vmem, vmem, vmem, pl.BlockSpec(memory_space=pltpu.SMEM), anywhere,
        ],
        out_specs=vmem,
        scratch_shapes=[
            pltpu.VMEM((SLOTS, 2, PIECE, 512), bf16),
            pltpu.VMEM((UNITS * PIECE, HID), bf16),
            pltpu.VMEM((UNITS * PIECE, HID), bf16),
            pltpu.VMEM((UNITS * PIECE, HID), bf16),
            pltpu.VMEM((3 * STAGE * PIECE, HID), bf16),
            pltpu.VMEM(((OWN + DEV * CAP) // BLK, BLK, HID), bf16),
            pltpu.VMEM((DEV * CAP, HID), bf16),
            pltpu.VMEM((16, 12, BLK, BLK), bf16),
            pltpu.VMEM((CAP, DEV), jnp.float32),
            pltpu.SemaphoreType.DMA((SLOTS,)),
            pltpu.SemaphoreType.DMA,
            pltpu.SemaphoreType.DMA((UNITS,)),
            pltpu.SemaphoreType.DMA,
            pltpu.SemaphoreType.DMA((3 * STAGE,)),
            pltpu.SemaphoreType.DMA,
            pltpu.SemaphoreType.DMA,
            pltpu.SemaphoreType.DMA,
            pltpu.SemaphoreType.DMA,
            pltpu.SemaphoreType.REGULAR((3,)),
        ],
        compiler_params=pltpu.CompilerParams(
            collective_id=0, has_side_effects=True, vmem_limit_bytes=56 * 1024 * 1024
        ),
        cost_estimate=pl.CostEstimate(
            flops=15_000_000_000, bytes_accessed=24 * 1024 * 1024, transcendentals=0
        ),
    )(
        features.reshape(8, OWN, 512), project, bias.reshape(1, HID), send_rows[0].T, send_count,
        block_ids.transpose(2, 0, 1), block_weights[0],
    )
    return jnp.maximum(summed, 0)


def solution(mesh):
    placed = (
        P("bulk", "feat"),
        P("feat", None),
        P(),
        P(("feat", "bulk"), None, None),
        P(("feat", "bulk"), None),
        P(("feat", "bulk"), None, None),
        P(("feat", "bulk"), None, None, None, None),
    )
    return jax.shard_map(
        per_device, mesh=mesh, in_specs=placed, out_specs=P(("bulk", "feat"), None), check_vma=False
    )
```
